32 devices in a mesh: groups: 2 (over x), replica: 16 (over z, y, core).
Axes of the slice: x: 2, y: 2, z: 4, core: 2. Of those that a mesh axis runs over, the one named last changes fastest.
Arguments:
- inputs: bfloat16 [2, 1024, 8192], P(None, ('groups', 'replica')), parts along dimension 1, may hold values from -6 to 6
- query_weight: bfloat16 [8192, 512], replicated, may hold values from -0.0625 to 0.0625
- key_cache: bfloat16 [1024, 128, 128], P(('groups', 'replica')), parts along dimension 0, may hold values from -1000 to 1000
- value_cache: bfloat16 [1024, 128, 128], P(('groups', 'replica')), parts along dimension 0, may hold values from -6 to 6
- cache_len: int32 [1024], P(('groups', 'replica')), parts along dimension 0, may hold values from 32 to 127
- adapter_ids: int32 [2, 1024, 1], P(None, ('groups', 'replica')), parts along dimension 1, may hold values from 0 to 15; in each aligned block of 32 rows (0 to 31, 32 to 63, ..., all dimensions but the last counted through in order) at most 2 rows name the same one
- adapter_home: int32 [16], P('replica'), may hold values from 0 to 15, each once
- shrink_pool: bfloat16 [16, 8192, 64], P('replica'), may hold values from -0.0625 to 0.0625
- expand_pool: bfloat16 [16, 64, 512], P('replica'), may hold values from -0.75 to 0.75
Outputs:
- attended: bfloat16 [2, 1024, 512], P(None, ('groups', 'replica')), parts along dimension 1
The draws below stay inside these ranges and needn't reach their ends.
There are 2 independent parts, one for each index of `groups`. The reference program is written for one: setup_inputs(seed, part) draws one part's arguments, and reference() takes and returns one part's arrays. A program takes and returns all parts, laid end to end along the dimension named above; an argument that names none is the same for every part. Nothing has to cross between parts.
Inputs may be any that keep to these rules, and one draw needn't show every extreme that they name: `adapter_ids`: in the rows of one replica at one step no adapter is named more than 2 times, a bound that some adapter reaches in some of these blocks.
All inputs are finite; a program needn't handle non-finite values.
Results may differ from the reference program's by a relative error of at most 0.012.
The reference program's roundings to bfloat16 on the way count: a program that leaves them out, or rounds other values in their place, can miss the bound.
Values may be sent and summed in bfloat16 or wider, within the bound.
A program may use at most 64 MiB of HBM per device.

```python
import math
import jax
import jax.numpy as jnp
import numpy as np
from jax import lax

D = 8192
HEAD = 128
RANK = 64
ROWS = 32
CTX = 128
STEPS = 2
MOST = 2
QW = 512
TOKS = 512
ADAPTERS = 16


def draw_key_cache(key, part):
    key = jax.random.fold_in(key, 11)
    first_key = jax.random.fold_in(key, 0)
    cache = jnp.clip(jax.random.normal(first_key, (TOKS, CTX, HEAD), jnp.float32), -6.0, 6.0)
    return cache.astype(jnp.bfloat16)


def touch_ends(array, rng, least, high):
    dims = array.shape
    place = [jax.random.randint(jax.random.fold_in(rng, axis), (), 0, dims[axis]) for axis in range(len(dims))]
    array = array.at[tuple(place)].set(least)
    longest = dims.index(max(dims))
    place[longest] = (place[longest] + 1) % dims[longest]
    return array.at[tuple(place)].set(high)


def level_of(stream_key, shape, pieces, least, largest):
    gain, own = 1.0, jax.random.fold_in(stream_key, 6)
    for position, parts in pieces:
        heights = jnp.exp(jax.random.uniform(jax.random.fold_in(own, position), (parts,), jnp.float32, least / len(pieces), largest / len(pieces)))
        gain = gain * jnp.repeat(heights, shape[position] // parts).reshape([-1 if axis == position else 1 for axis in range(len(shape))])
    return gain


def routed_block(key, own, number, rows, count, top, limit, lean):
    ranking = jax.random.permutation(key, count)
    packed, common = portions_of(count, rows * top, limit, lean, True), portions_of(count, rows * top, limit, lean, False)
    places = jnp.arange(count)

    def named(sizes, rotation):
        used = int((sizes > 0).sum())
        fixed = max(1, used // 4)
        moved = fixed + (places - fixed + rotation * (used - fixed)) % max(1, count - fixed)
        return jnp.zeros((count,), jnp.int32).at[ranking[jnp.where(places < fixed, places, moved)]].set(jnp.asarray(sizes, jnp.int32))

    sizes = jnp.where(number % 4 == 0, named(packed, number // 4), named(common, number - number // 4 - 1))
    mixed = jax.random.permutation(jax.random.fold_in(own, 3), count)
    source_of, taker = mixed[0:count // 2 * 2:2], mixed[1:count // 2 * 2:2]
    margin = jnp.minimum(sizes[source_of] - 1, limit - sizes[taker]) // 2
    margin = jnp.where((source_of == ranking[0]) | (taker == ranking[0]) | (sizes[taker] == 0), 0, jnp.maximum(margin, 0))
    moved = jax.random.randint(jax.random.fold_in(own, 4), (count // 2,), 0, 1 << 20) % (margin + 1)
    sizes = sizes.at[source_of].add(-moved).at[taker].add(moved)
    items = jnp.searchsorted(jnp.cumsum(sizes), jnp.arange(rows * top), side="right").astype(jnp.int32)
    listing = items.reshape(top, rows).T
    listing = listing[jax.random.permutation(jax.random.fold_in(own, 1), rows)]
    rotation = jax.random.randint(jax.random.fold_in(own, 2), (rows, 1), 0, top)
    return jnp.take_along_axis(listing, (jnp.arange(top)[None, :] + rotation) % top, axis=1)


def portions_of(number_of, total, reach, slope, full):
    weights = [(1 << 20) // math.isqrt(standing ** slope) + 1 for standing in range(1, number_of + 1)]
    largest = reach if full else min(reach, max(-(-total // number_of), total * weights[0] // sum(weights)))
    least = 1 if total - largest >= number_of - 1 else 0
    given, rest = [largest] + [least] * (number_of - 1), total - largest - least * (number_of - 1)
    while rest > 0:
        movable = [i for i in range(1, number_of) if given[i] < largest] or [i for i in range(1, number_of) if given[i] < reach]
        pool, remaining = sum([weights[i] for i in movable]), rest
        for i in movable:
            extra = min(reach - given[i], max(1, remaining * weights[i] // pool), rest)
            given[i] = given[i] + extra
            rest = rest - extra
    return np.array(given)


def gaussian(stream_key, shape, deviation, reach, cuts=(), kind=jnp.bfloat16):
    drawn = jax.random.normal(stream_key, shape, jnp.float32) * deviation
    if len(cuts) > 0:
        drawn = level_of(stream_key, shape, cuts, -0.22, 0.18) * drawn
    return jnp.clip(drawn, min=-reach, max=reach).astype(kind)


def setup_inputs(seed: int = 0, part: int = 0) -> dict:
    key_of = jax.random.split(jax.random.key(seed), 10)
    own_keys = jax.random.split(jax.random.fold_in(key_of[9], part), 10)
    inputs = gaussian(own_keys[0], (STEPS, TOKS, D), 1.0, 6.0, ((1, 16),))
    query_weight = gaussian(key_of[1], (D, QW), D ** -0.5, 0.0625)
    key_cache = draw_key_cache(jax.random.fold_in(jax.random.fold_in(key_of[9], part), 71), part)
    value_cache = gaussian(own_keys[3], (TOKS, CTX, HEAD), 1.0, 6.0, ((0, 16),))
    cache_len = touch_ends(jax.random.randint(own_keys[4], (TOKS,), CTX // 4, CTX), jax.random.fold_in(own_keys[4], 1), CTX // 4, CTX - 1).astype(jnp.int32)
    adapter_ids_keys = jax.random.split(jax.random.fold_in(own_keys[5], 1), STEPS * TOKS // ROWS)
    adapter_ids_turns = jax.random.permutation(jax.random.fold_in(own_keys[5], 3), STEPS * TOKS // ROWS)
    adapter_ids = jax.vmap(lambda own, number: routed_block(jax.random.fold_in(own_keys[5], 2), own, number, ROWS, ADAPTERS, 1, MOST, 2))(adapter_ids_keys, adapter_ids_turns).reshape((STEPS, TOKS, 1))
    adapter_home = jax.random.permutation(key_of[6], ADAPTERS).astype(jnp.int32)
    shrink_pool = gaussian(key_of[7], (ADAPTERS, D, RANK), D ** -0.5, 0.0625, ((0, 16),))
    expand_pool = gaussian(key_of[8], (ADAPTERS, RANK, QW), RANK ** -0.5, 0.75, ((0, 16),))
    return dict(inputs=inputs, query_weight=query_weight, key_cache=key_cache, value_cache=value_cache, cache_len=cache_len, adapter_ids=adapter_ids, adapter_home=adapter_home, shrink_pool=shrink_pool, expand_pool=expand_pool)


def attention(query_vectors, key_cache, value_cache, limits):
    total_row_count = query_vectors.shape[0]
    per_head = query_vectors.reshape(total_row_count, -1, HEAD).astype(jnp.float32)
    scores = jnp.einsum('nhd,ncd->nhc', per_head, key_cache.astype(jnp.float32)) * (HEAD ** -0.5)
    positions = jnp.arange(CTX, dtype=jnp.int32)
    visible = positions[None, None, :] < limits[:, None, None]
    scores = jnp.where(visible, scores, -1e30)
    highest = jnp.max(scores, axis=-1, keepdims=True)
    weights = jnp.exp(scores - highest)
    weights = (weights / jnp.sum(weights, axis=-1, keepdims=True)).astype(jnp.bfloat16)
    mixed = jnp.einsum('nhc,ncd->nhd', weights.astype(jnp.float32), value_cache.astype(jnp.float32))
    return mixed.astype(jnp.bfloat16).reshape(total_row_count, -1)


def reference(inputs, query_weight, key_cache, value_cache, cache_len, adapter_ids, adapter_home, shrink_pool, expand_pool):
    outputs = []
    for step_index in range(STEPS):
        decode_step_rows = inputs[step_index]
        plain_query_rows = jnp.dot(decode_step_rows, query_weight, preferred_element_type=jnp.float32)
        adapter_pool_entries = jnp.take(adapter_home, adapter_ids[step_index, :, 0], axis=0).astype(jnp.int32)

        def lone_token_row(row_pair):
            token_row, pool_slot = row_pair
            shrink = lax.dynamic_index_in_dim(shrink_pool, pool_slot, 0, keepdims=False)
            expand = lax.dynamic_index_in_dim(expand_pool, pool_slot, 0, keepdims=False)
            low_rank = jnp.dot(token_row, shrink, preferred_element_type=jnp.float32).astype(jnp.bfloat16)
            return jnp.dot(low_rank, expand, preferred_element_type=jnp.float32).astype(jnp.bfloat16)

        adapter_correction = lax.map(lone_token_row, (decode_step_rows, adapter_pool_entries))
        query_vectors = (plain_query_rows + adapter_correction.astype(jnp.float32)).astype(jnp.bfloat16)
        outputs.append(attention(query_vectors, key_cache, value_cache, cache_len + step_index))
    return jnp.stack(outputs)
```

```python
import functools

import jax
import jax.numpy as jnp
from jax import lax
from jax.experimental import pallas as pl
from jax.experimental.pallas import tpu as pltpu
from jax.sharding import PartitionSpec as P

HEAD = 128
MOST = 2
MESH = pl.DeviceIdType.MESH
F32 = jnp.float32
BF16 = jnp.bfloat16


def iota(shape, axis):
    return lax.broadcasted_iota(jnp.int32, shape, axis)


def kernel(
    peers,
    steps,
    rows,
    width,
    rank,
    features,
    ctx,
    x_hbm,
    w_hbm,
    k_hbm,
    v_hbm,
    len_ref,
    ids_ref,
    home_ref,
    shrink_hbm,
    expand_ref,
    o_ref,
    x,
    w,
    k,
    v,
    shrink,
    wide,
    home_src,
    homes,
    out,
    inbox,
    ans_out,
    ans_in,
    base,
    limits,
    mixed,
    local_sem,
    w_sem,
    home_send,
    home_recv,
    row_send,
    row_recv,
    ans_send,
    ans_recv,
):
    me = lax.axis_index("replica")
    heads = features // HEAD
    parts = 16 // MOST
    cols = width // parts
    per_row = steps * heads
    half = peers // 2
    w_parts = w_sem.shape[0]
    w_rows = width // w_parts

    def offset(i):
        return lax.rem(peers // 2 + (1 - 2 * lax.rem(i, 2)) * ((i + 1) // 2) + peers, peers)

    def target(i):
        return lax.rem(me + offset(i), peers)

    def source(i):
        return lax.rem(me - offset(i) + peers, peers)

    def w_copy(c):
        piece = pl.ds(c * w_rows, w_rows)
        return pltpu.make_async_copy(w_hbm.at[piece], w.at[piece], w_sem.at[c])

    x_copy = pltpu.make_async_copy(x_hbm, x, local_sem.at[0])
    shrink_copy = pltpu.make_async_copy(shrink_hbm, shrink, local_sem.at[1])
    k_copy = pltpu.make_async_copy(k_hbm, k, local_sem.at[2])
    v_copy = pltpu.make_async_copy(v_hbm, v, local_sem.at[3])

    x_copy.start()
    barrier = pltpu.get_barrier_semaphore()

    @pl.loop(0, peers - 1)
    def _(i):
        pl.semaphore_signal(barrier, inc=1, device_id={"replica": target(i)}, device_id_type=MESH)

    for c in range(w_parts):
        w_copy(c).start()
    shrink_copy.start()
    k_copy.start()
    v_copy.start()
    home_src[...] = jnp.full(home_src.shape, home_ref[0], jnp.int32)
    homes[me] = home_src[...]

    def home_copy(i, slot):
        return pltpu.make_async_remote_copy(
            src_ref=home_src,
            dst_ref=homes.at[slot],
            send_sem=home_send.at[i],
            recv_sem=home_recv.at[slot],
            device_id={"replica": target(i)},
            device_id_type=MESH,
        )

    pl.semaphore_wait(barrier, peers - 1)

    @pl.loop(0, peers - 1)
    def _(i):
        home_copy(i, me).start()

    total = steps * rows
    ids_col = ids_ref[...].reshape(total, 1).astype(F32)

    def along(col, index):
        return jnp.sum(jnp.where(iota((total, index.shape[1]), 0) == index, col, 0.0), axis=0, keepdims=True)

    ids_row = along(ids_col, iota((1, total), 1))
    before = (iota((total, total), 1) < iota((total, total), 0)) & (
        iota((total, total), 1) // rows == iota((total, total), 0) // rows
    )
    place_col = jnp.sum(jnp.where(before & (ids_row == ids_col), 1.0, 0.0), axis=1, keepdims=True)
    lanes = iota((1, parts * rows), 1)
    pack_ids = [along(ids_col, lanes % rows + s * rows) for s in range(steps)]
    pack_place = [along(place_col, lanes % rows + s * rows) for s in range(steps)]
    block = iota((peers * 16, 1), 0)
    pack_target = target(block // 16)
    fits = [
        (block % parts == lanes // rows) & ((block // parts) % MOST == pack_place[s].astype(jnp.int32))
        for s in range(steps)
    ]
    x_copy.wait()

    @pl.loop(0, peers - 1)
    def _(i):
        home_copy(i, source(i)).wait_recv()

    home_col = jnp.max(homes[...], axis=1)[:, 0:1].astype(F32)

    def owner_of(ids):
        named = iota((peers, ids.shape[1]), 0) == ids.astype(jnp.int32)
        return jnp.sum(jnp.where(named, home_col, 0.0), axis=0, keepdims=True).astype(jnp.int32)

    def row_copy(s, i):
        place = pl.ds(s * 16, 16)
        return pltpu.make_async_remote_copy(
            src_ref=out.at[i, place],
            dst_ref=inbox.at[i, place],
            send_sem=row_send.at[s, i],
            recv_sem=row_recv.at[s, i],
            device_id={"replica": target(i)},
            device_id_type=MESH,
        )

    for s in range(steps):
        routing = jnp.where(fits[s] & (pack_target == owner_of(pack_ids[s])), 1.0, 0.0).astype(BF16)
        tall = jnp.concatenate([x[s, :, c * cols : (c + 1) * cols] for c in range(parts)], axis=0)
        packed = jnp.dot(routing, tall, preferred_element_type=F32).astype(BF16)
        packed = packed.reshape(peers, 16, cols)
        out[:, s * 16 : (s + 1) * 16, :] = packed
        inbox[peers - 1, s * 16 : (s + 1) * 16, :] = packed[peers - 1]

        @pl.loop(0, peers - 1)
        def _(i):
            row_copy(s, i).start()

    q_lanes = iota((1, rows * per_row), 1)
    q_rows = q_lanes // per_row + ((q_lanes // heads) % steps) * rows
    q_owner = owner_of(along(ids_col, q_rows))
    q_place = along(place_col, q_rows).astype(jnp.int32)
    a_rows = iota((peers * steps * MOST * heads, 1), 0)
    per_peer = steps * MOST * heads
    back = (
        (target(a_rows // per_peer) == q_owner)
        & ((a_rows // (MOST * heads)) % steps == (q_lanes // heads) % steps)
        & ((a_rows // heads) % MOST == q_place)
        & (a_rows % heads == q_lanes % heads)
    )
    back = jnp.transpose(jnp.where(back, 1.0, 0.0)).astype(BF16)

    flat = jnp.zeros((total, features), F32)
    for c in range(w_parts):
        w_copy(c).wait()
        piece = x[:, :, c * w_rows : (c + 1) * w_rows].reshape(total, w_rows)
        flat = flat + jnp.dot(piece, w[c * w_rows : (c + 1) * w_rows], preferred_element_type=F32)
    for s in range(steps):
        for h in range(heads):
            base[pl.ds(s * heads + h, rows, stride=per_row), :] = flat[
                s * rows : (s + 1) * rows, h * HEAD : (h + 1) * HEAD
            ]
    step_of = iota((per_row, ctx), 0) // heads
    for t in range(rows):
        limits[t] = step_of + len_ref[t]
    shrink_copy.wait()
    for c in range(0, parts, 2):
        wide[:, c * rank : (c + 2) * rank] = jnp.concatenate(
            [shrink[0, c * cols : (c + 1) * cols], shrink[0, (c + 1) * cols : (c + 2) * cols]], axis=1
        )
    expand = expand_ref[0]
    expand_tall = jnp.concatenate([expand[:, h * HEAD : (h + 1) * HEAD] for h in range(heads)], axis=0)
    k_copy.wait()
    v_copy.wait()

    g_rows = half * 16
    own_part = iota((g_rows, parts * rank), 0) % parts == iota((g_rows, parts * rank), 1) // rank

    def low_rank(s, g):
        block = inbox[g * half : (g + 1) * half, s * 16 : (s + 1) * 16, :].reshape(g_rows, cols)
        full = jnp.dot(block, wide[...], preferred_element_type=F32)
        full = jnp.where(own_part, full, 0.0).reshape(g_rows // parts, parts, parts * rank)
        full = jnp.sum(full, axis=1)
        while full.shape[1] > 2 * rank:
            full = full[:, : full.shape[1] // 2] + full[:, full.shape[1] // 2 :]
        return (full + pltpu.roll(full, rank, 1)).astype(BF16)

    def wait_rows(s, g):
        @pl.loop(g * half, min((g + 1) * half, peers - 1))
        def _(i):
            row_copy(s, i).wait_recv()

    def answer_copy(i, to):
        return pltpu.make_async_remote_copy(
            src_ref=ans_out.at[i],
            dst_ref=ans_in.at[i],
            send_sem=ans_send.at[i],
            recv_sem=ans_recv.at[i],
            device_id={"replica": to},
            device_id_type=MESH,
        )

    lows = {}
    r_rows = half * per_peer
    r_from = iota((r_rows, steps * half * MOST), 1)
    r_to = iota((r_rows, steps * half * MOST), 0)
    spread = (
        ((r_to // (MOST * heads)) % steps == r_from // (half * MOST))
        & (r_to // per_peer == (r_from // MOST) % half)
        & ((r_to // heads) % MOST == r_from % MOST)
    )
    spread = jnp.where(spread, 1.0, 0.0).astype(BF16)
    own_head = iota((r_rows, heads * rank), 0) % heads == iota((r_rows, heads * rank), 1) // rank
    for s in range(steps):
        for g in range(2):
            wait_rows(s, g)
            lows[s, g] = low_rank(s, g)
            if s < steps - 1:
                continue
            low = jnp.concatenate([lows[q, g] for q in range(steps)], axis=0)
            low = jnp.concatenate([low] * (heads // 2), axis=1)
            low = jnp.dot(spread, low, preferred_element_type=F32)
            low = jnp.where(own_head, low, 0.0).astype(BF16)
            answer = jnp.dot(low, expand_tall, preferred_element_type=F32).astype(BF16)
            answer = answer.reshape(half, per_peer, HEAD)
            ans_out[g * half : (g + 1) * half] = answer
            if g == 1:
                ans_in[peers - 1] = answer[half - 1]

            @pl.loop(g * half, min((g + 1) * half, peers - 1))
            def _(i):
                answer_copy(i, source(i)).start()

    @pl.loop(0, peers - 1)
    def _(i):
        answer_copy(i, source(i)).wait_recv()

    delta = jnp.dot(back, ans_in[...].reshape(peers * per_peer, HEAD), preferred_element_type=F32)
    query = (base[...] + delta).astype(BF16).reshape(rows, per_row, HEAD)
    scores = lax.dot_general(query, k[...], (((2,), (2,)), ((0,), (0,))), preferred_element_type=F32)
    scores = scores * HEAD ** (-0.5)
    scores = jnp.where(iota((rows, per_row, ctx), 2) < limits[...], scores, -1e30)
    weights = jnp.exp(scores - jnp.max(scores, axis=-1, keepdims=True))
    weights = (weights / jnp.sum(weights, axis=-1, keepdims=True)).astype(BF16)
    result = lax.dot_general(weights, v[...], (((2,), (1,)), ((0,), (0,))), preferred_element_type=F32)
    mixed[...] = result.reshape(rows * per_row, HEAD)
    for s in range(steps):
        for h in range(heads):
            o_ref[s, :, h * HEAD : (h + 1) * HEAD] = mixed[
                pl.ds(s * heads + h, rows, stride=per_row), :
            ].astype(BF16)

    @pl.loop(0, peers - 1)
    def _(i):
        home_copy(i, me).wait_send()
        for s in range(steps):
            row_copy(s, i).wait_send()
        answer_copy(i, source(i)).wait_send()


def body(inputs, query_weight, key_cache, value_cache, cache_len, ids, home, shrink_pool, expand_pool):
    peers = lax.axis_size("replica")
    steps, rows, width = inputs.shape
    features = query_weight.shape[1]
    rank = shrink_pool.shape[2]
    ctx = key_cache.shape[1]
    heads = features // HEAD
    cols = width * MOST // 16
    per_row = steps * heads
    vmem = pl.BlockSpec(memory_space=pltpu.VMEM)
    smem = pl.BlockSpec(memory_space=pltpu.SMEM)
    hbm = pl.BlockSpec(memory_space=pl.ANY)
    dma = pltpu.SemaphoreType.DMA
    return pl.pallas_call(
        functools.partial(kernel, peers, steps, rows, width, rank, features, ctx),
        out_shape=jax.ShapeDtypeStruct((steps, rows, features), BF16),
        in_specs=[hbm, hbm, hbm, hbm, smem, vmem, smem, hbm, vmem],
        out_specs=vmem,
        scratch_shapes=[
            pltpu.VMEM(inputs.shape, BF16),
            pltpu.VMEM(query_weight.shape, BF16),
            pltpu.VMEM(key_cache.shape, BF16),
            pltpu.VMEM(value_cache.shape, BF16),
            pltpu.VMEM(shrink_pool.shape, BF16),
            pltpu.VMEM((cols, rank * 16 // MOST), BF16),
            pltpu.VMEM((8, 128), jnp.int32),
            pltpu.VMEM((peers, 8, 128), jnp.int32),
            pltpu.VMEM((peers, steps * 16, cols), BF16),
            pltpu.VMEM((peers, steps * 16, cols), BF16),
            pltpu.VMEM((peers, steps * MOST * heads, HEAD), BF16),
            pltpu.VMEM((peers, steps * MOST * heads, HEAD), BF16),
            pltpu.VMEM((rows * per_row, HEAD), F32),
            pltpu.VMEM((rows, per_row, ctx), jnp.int32),
            pltpu.VMEM((rows * per_row, HEAD), F32),
            dma((4,)),
            dma((8,)),
            dma((peers,)),
            dma((peers,)),
            dma((steps, peers)),
            dma((steps, peers)),
            dma((peers,)),
            dma((peers,)),
        ],
        compiler_params=pltpu.CompilerParams(
            collective_id=0, has_side_effects=True, vmem_limit_bytes=48 * 2**20
        ),
    )(inputs, query_weight, key_cache, value_cache, cache_len, ids, home, shrink_pool, expand_pool)


def solution(mesh):
    return jax.shard_map(
        body,
        mesh=mesh,
        in_specs=(
            P(None, ("groups", "replica"), None),
            P(),
            P(("groups", "replica"), None, None),
            P(("groups", "replica"), None, None),
            P(("groups", "replica")),
            P(None, ("groups", "replica"), None),
            P("replica"),
            P("replica", None, None),
            P("replica", None, None),
        ),
        out_specs=P(None, ("groups", "replica"), None),
        check_vma=False,
    )
```

```python
import functools

import jax
import jax.numpy as jnp
from jax import lax
from jax.experimental import pallas as pl
from jax.experimental.pallas import tpu as pltpu
from jax.sharding import PartitionSpec as P

HEAD = 128
MOST = 2
MESH = pl.DeviceIdType.MESH
F32 = jnp.float32
BF16 = jnp.bfloat16


def iota(shape, axis):
    return lax.broadcasted_iota(jnp.int32, shape, axis)


def kernel(
    peers,
    steps,
    rows,
    width,
    rank,
    features,
    ctx,
    x_hbm,
    w_hbm,
    k_hbm,
    v_hbm,
    len_hbm,
    ids_hbm,
    home_hbm,
    shrink_hbm,
    expand_hbm,
    o_ref,
    x,
    w,
    k,
    v,
    len_ref,
    ids_ref,
    home_ref,
    shrink,
    expand_ref,
    wide,
    home_src,
    homes,
    out,
    inbox,
    ans_out,
    ans_in,
    base,
    limits,
    mixed,
    local_sem,
    w_sem,
    home_send,
    home_recv,
    row_send,
    row_recv,
    ans_send,
    ans_recv,
):
    me = lax.axis_index("replica")
    heads = features // HEAD
    parts = 16 // MOST
    cols = width // parts
    per_row = steps * heads
    half = peers // 2
    w_parts = w_sem.shape[0]
    w_rows = width // w_parts

    def offset(i):
        return lax.rem(peers // 2 + (1 - 2 * lax.rem(i, 2)) * ((i + 1) // 2) + peers, peers)

    def target(i):
        return lax.rem(me + offset(i), peers)

    def source(i):
        return lax.rem(me - offset(i) + peers, peers)

    def w_copy(c):
        piece = pl.ds(c * w_rows, w_rows)
        return pltpu.make_async_copy(w_hbm.at[piece], w.at[piece], w_sem.at[c])

    x_copy = pltpu.make_async_copy(x_hbm, x, local_sem.at[0])
    shrink_copy = pltpu.make_async_copy(shrink_hbm, shrink, local_sem.at[1])
    k_copy = pltpu.make_async_copy(k_hbm, k, local_sem.at[2])
    v_copy = pltpu.make_async_copy(v_hbm, v, local_sem.at[3])

    home_local = pltpu.make_async_copy(home_hbm, home_ref, local_sem.at[4])
    ids_copy = pltpu.make_async_copy(ids_hbm, ids_ref, local_sem.at[5])
    len_copy = pltpu.make_async_copy(len_hbm, len_ref, local_sem.at[6])
    expand_copy = pltpu.make_async_copy(expand_hbm, expand_ref, local_sem.at[7])

    home_local.start()
    ids_copy.start()
    x_copy.start()
    barrier = pltpu.get_barrier_semaphore()

    @pl.loop(0, peers - 1)
    def _(i):
        pl.semaphore_signal(barrier, inc=1, device_id={"replica": target(i)}, device_id_type=MESH)

    for c in range(w_parts):
        w_copy(c).start()
    shrink_copy.start()
    k_copy.start()
    v_copy.start()
    len_copy.start()
    expand_copy.start()
    home_local.wait()
    home_src[...] = jnp.full(home_src.shape, home_ref[0], jnp.int32)
    homes[me] = home_src[...]

    def home_copy(i, slot):
        return pltpu.make_async_remote_copy(
            src_ref=home_src,
            dst_ref=homes.at[slot],
            send_sem=home_send.at[i],
            recv_sem=home_recv.at[slot],
            device_id={"replica": target(i)},
            device_id_type=MESH,
        )

    pl.semaphore_wait(barrier, peers - 1)

    @pl.loop(0, peers - 1)
    def _(i):
        home_copy(i, me).start()

    total = steps * rows
    ids_copy.wait()
    same = iota((rows, rows), 0) == iota((rows, rows), 1)
    ids_col = jnp.concatenate(
        [
            jnp.sum(jnp.where(same, ids_ref[s].astype(F32), 0.0), axis=1, keepdims=True)
            for s in range(steps)
        ],
        axis=0,
    )

    def along(col, index):
        return jnp.sum(jnp.where(iota((total, index.shape[1]), 0) == index, col, 0.0), axis=0, keepdims=True)

    ids_row = along(ids_col, iota((1, total), 1))
    before = (iota((total, total), 1) < iota((total, total), 0)) & (
        iota((total, total), 1) // rows == iota((total, total), 0) // rows
    )
    place_col = jnp.sum(jnp.where(before & (ids_row == ids_col), 1.0, 0.0), axis=1, keepdims=True)
    lanes = iota((1, parts * rows), 1)
    pack_ids = [along(ids_col, lanes % rows + s * rows) for s in range(steps)]
    pack_place = [along(place_col, lanes % rows + s * rows) for s in range(steps)]
    block = iota((peers * 16, 1), 0)
    pack_target = target(block // 16)
    fits = [
        (block % parts == lanes // rows) & ((block // parts) % MOST == pack_place[s].astype(jnp.int32))
        for s in range(steps)
    ]
    x_copy.wait()

    @pl.loop(0, peers - 1)
    def _(i):
        home_copy(i, source(i)).wait_recv()

    home_col = jnp.max(homes[...], axis=1)[:, 0:1].astype(F32)

    def owner_of(ids):
        named = iota((peers, ids.shape[1]), 0) == ids.astype(jnp.int32)
        return jnp.sum(jnp.where(named, home_col, 0.0), axis=0, keepdims=True).astype(jnp.int32)

    def row_copy(s, i):
        place = pl.ds(s * 16, 16)
        return pltpu.make_async_remote_copy(
            src_ref=out.at[i, place],
            dst_ref=inbox.at[i, place],
            send_sem=row_send.at[s, i],
            recv_sem=row_recv.at[s, i],
            device_id={"replica": target(i)},
            device_id_type=MESH,
        )

    for s in range(steps):
        routing = jnp.where(fits[s] & (pack_target == owner_of(pack_ids[s])), 1.0, 0.0).astype(BF16)
        tall = jnp.concatenate([x[s, :, c * cols : (c + 1) * cols] for c in range(parts)], axis=0)
        packed = jnp.dot(routing, tall, preferred_element_type=F32).astype(BF16)
        packed = packed.reshape(peers, 16, cols)
        out[:, s * 16 : (s + 1) * 16, :] = packed
        inbox[peers - 1, s * 16 : (s + 1) * 16, :] = packed[peers - 1]

        @pl.loop(0, peers - 1)
        def _(i):
            row_copy(s, i).start()

    q_lanes = iota((1, rows * per_row), 1)
    q_rows = q_lanes // per_row + ((q_lanes // heads) % steps) * rows
    q_owner = owner_of(along(ids_col, q_rows))
    q_place = along(place_col, q_rows).astype(jnp.int32)
    a_rows = iota((peers * steps * MOST * heads, 1), 0)
    per_peer = steps * MOST * heads
    back = (
        (target(a_rows // per_peer) == q_owner)
        & ((a_rows // (MOST * heads)) % steps == (q_lanes // heads) % steps)
        & ((a_rows // heads) % MOST == q_place)
        & (a_rows % heads == q_lanes % heads)
    )
    back = jnp.transpose(jnp.where(back, 1.0, 0.0)).astype(BF16)

    flat = jnp.zeros((total, features), F32)
    for c in range(w_parts):
        w_copy(c).wait()
        piece = x[:, :, c * w_rows : (c + 1) * w_rows].reshape(total, w_rows)
        flat = flat + jnp.dot(piece, w[c * w_rows : (c + 1) * w_rows], preferred_element_type=F32)
    for s in range(steps):
        for h in range(heads):
            base[pl.ds(s * heads + h, rows, stride=per_row), :] = flat[
                s * rows : (s + 1) * rows, h * HEAD : (h + 1) * HEAD
            ]
    step_of = iota((per_row, ctx), 0) // heads
    len_copy.wait()
    for t in range(rows):
        limits[t] = step_of + len_ref[t]
    shrink_copy.wait()
    for c in range(parts):
        wide[c * rank : (c + 1) * rank] = shrink[0, :, c * cols : (c + 1) * cols]
    expand_copy.wait()
    expand = expand_ref[0]
    expand_tall = jnp.concatenate([expand[:, h * HEAD : (h + 1) * HEAD] for h in range(heads)], axis=0)
    k_copy.wait()
    v_copy.wait()

    g_rows = half * 16
    own_part = iota((g_rows, parts * rank), 0) % parts == iota((g_rows, parts * rank), 1) // rank

    def low_rank(s, g):
        block = inbox[g * half : (g + 1) * half, s * 16 : (s + 1) * 16, :].reshape(g_rows, cols)
        full = lax.dot_general(block, wide[...], (((1,), (1,)), ((), ())), preferred_element_type=F32)
        full = jnp.where(own_part, full, 0.0).reshape(g_rows // parts, parts, parts * rank)
        full = jnp.sum(full, axis=1)
        while full.shape[1] > 2 * rank:
            full = full[:, : full.shape[1] // 2] + full[:, full.shape[1] // 2 :]
        return (full + pltpu.roll(full, rank, 1)).astype(BF16)

    def wait_rows(s, g):
        @pl.loop(g * half, min((g + 1) * half, peers - 1))
        def _(i):
            row_copy(s, i).wait_recv()

    def answer_copy(i, to):
        return pltpu.make_async_remote_copy(
            src_ref=ans_out.at[i],
            dst_ref=ans_in.at[i],
            send_sem=ans_send.at[i],
            recv_sem=ans_recv.at[i],
            device_id={"replica": to},
            device_id_type=MESH,
        )

    lows = {}
    r_rows = half * per_peer
    r_from = iota((r_rows, steps * half * MOST), 1)
    r_to = iota((r_rows, steps * half * MOST), 0)
    spread = (
        ((r_to // (MOST * heads)) % steps == r_from // (half * MOST))
        & (r_to // per_peer == (r_from // MOST) % half)
        & ((r_to // heads) % MOST == r_from % MOST)
    )
    spread = jnp.where(spread, 1.0, 0.0).astype(BF16)
    own_head = iota((r_rows, heads * rank), 0) % heads == iota((r_rows, heads * rank), 1) // rank
    for s in range(steps):
        for g in range(2):
            wait_rows(s, g)
            lows[s, g] = low_rank(s, g)
            if s < steps - 1:
                continue
            low = jnp.concatenate([lows[q, g] for q in range(steps)], axis=0)
            low = jnp.concatenate([low] * (heads // 2), axis=1)
            low = jnp.dot(spread, low, preferred_element_type=F32)
            low = jnp.where(own_head, low, 0.0).astype(BF16)
            answer = jnp.dot(low, expand_tall, preferred_element_type=F32).astype(BF16)
            answer = answer.reshape(half, per_peer, HEAD)
            ans_out[g * half : (g + 1) * half] = answer
            if g == 1:
                ans_in[peers - 1] = answer[half - 1]

            @pl.loop(g * half, min((g + 1) * half, peers - 1))
            def _(i):
                answer_copy(i, source(i)).start()

    @pl.loop(0, peers - 1)
    def _(i):
        answer_copy(i, source(i)).wait_recv()

    delta = jnp.dot(back, ans_in[...].reshape(peers * per_peer, HEAD), preferred_element_type=F32)
    query = (base[...] + delta).astype(BF16).reshape(rows, per_row, HEAD)
    scores = lax.dot_general(query, k[...], (((2,), (2,)), ((0,), (0,))), preferred_element_type=F32)
    scores = scores * HEAD ** (-0.5)
    scores = jnp.where(iota((rows, per_row, ctx), 2) < limits[...], scores, -1e30)
    weights = jnp.exp(scores - jnp.max(scores, axis=-1, keepdims=True))
    weights = (weights / jnp.sum(weights, axis=-1, keepdims=True)).astype(BF16)
    result = lax.dot_general(weights, v[...], (((2,), (1,)), ((0,), (0,))), preferred_element_type=F32)
    mixed[...] = result.reshape(rows * per_row, HEAD)
    for s in range(steps):
        for h in range(heads):
            o_ref[s, :, h * HEAD : (h + 1) * HEAD] = mixed[
                pl.ds(s * heads + h, rows, stride=per_row), :
            ].astype(BF16)

    @pl.loop(0, peers - 1)
    def _(i):
        home_copy(i, me).wait_send()
        for s in range(steps):
            row_copy(s, i).wait_send()
        answer_copy(i, source(i)).wait_send()


def body(inputs, query_weight, key_cache, value_cache, cache_len, ids, home, shrink_pool, expand_pool):
    peers = lax.axis_size("replica")
    steps, rows, width = inputs.shape
    features = query_weight.shape[1]
    rank = shrink_pool.shape[2]
    ctx = key_cache.shape[1]
    heads = features // HEAD
    cols = width * MOST // 16
    per_row = steps * heads
    vmem = pl.BlockSpec(memory_space=pltpu.VMEM)
    hbm = pl.BlockSpec(memory_space=pltpu.HBM)
    dma = pltpu.SemaphoreType.DMA
    return pl.pallas_call(
        functools.partial(kernel, peers, steps, rows, width, rank, features, ctx),
        out_shape=jax.ShapeDtypeStruct((steps, rows, features), BF16),
        in_specs=[hbm] * 9,
        out_specs=vmem,
        scratch_shapes=[
            pltpu.VMEM(inputs.shape, BF16),
            pltpu.VMEM(query_weight.shape, BF16),
            pltpu.VMEM(key_cache.shape, BF16),
            pltpu.VMEM(value_cache.shape, BF16),
            pltpu.SMEM(cache_len.shape, jnp.int32),
            pltpu.VMEM((steps, 1, rows), jnp.int32),
            pltpu.SMEM(home.shape, jnp.int32),
            pltpu.VMEM((1, rank, width), BF16),
            pltpu.VMEM(expand_pool.shape, BF16),
            pltpu.VMEM((rank * 16 // MOST, cols), BF16),
            pltpu.VMEM((8, 128), jnp.int32),
            pltpu.VMEM((peers, 8, 128), jnp.int32),
            pltpu.VMEM((peers, steps * 16, cols), BF16),
            pltpu.VMEM((peers, steps * 16, cols), BF16),
            pltpu.VMEM((peers, steps * MOST * heads, HEAD), BF16),
            pltpu.VMEM((peers, steps * MOST * heads, HEAD), BF16),
            pltpu.VMEM((rows * per_row, HEAD), F32),
            pltpu.VMEM((rows, per_row, ctx), jnp.int32),
            pltpu.VMEM((rows * per_row, HEAD), F32),
            dma((8,)),
            dma((8,)),
            dma((peers,)),
            dma((peers,)),
            dma((steps, peers)),
            dma((steps, peers)),
            dma((peers,)),
            dma((peers,)),
        ],
        compiler_params=pltpu.CompilerParams(
            collective_id=0, has_side_effects=True, vmem_limit_bytes=60 * 2**20
        ),
    )(
        inputs,
        query_weight,
        key_cache,
        value_cache,
        cache_len,
        jnp.swapaxes(ids, 1, 2),
        home,
        jnp.swapaxes(shrink_pool, 1, 2),
        expand_pool,
    )


def solution(mesh):
    return jax.shard_map(
        body,
        mesh=mesh,
        in_specs=(
            P(None, ("groups", "replica"), None),
            P(),
            P(("groups", "replica"), None, None),
            P(("groups", "replica"), None, None),
            P(("groups", "replica")),
            P(None, ("groups", "replica"), None),
            P("replica"),
            P("replica", None, None),
            P("replica", None, None),
        ),
        out_specs=P(None, ("groups", "replica"), None),
        check_vma=False,
    )
```

```python
import functools

import jax
import jax.numpy as jnp
from jax import lax
from jax.experimental import pallas as pl
from jax.experimental.pallas import tpu as pltpu
from jax.sharding import PartitionSpec as P

HEAD = 128
MOST = 2
MESH = pl.DeviceIdType.MESH
F32 = jnp.float32
BF16 = jnp.bfloat16


def iota(shape, axis):
    return lax.broadcasted_iota(jnp.int32, shape, axis)


def kernel(
    peers,
    steps,
    rows,
    width,
    rank,
    features,
    ctx,
    x_hbm,
    w_hbm,
    k_hbm,
    v_hbm,
    len_hbm,
    ids_hbm,
    home_hbm,
    shrink_hbm,
    expand_hbm,
    o_ref,
    x,
    w,
    k,
    v,
    len_ref,
    ids_ref,
    home_ref,
    shrink,
    expand_ref,
    wide,
    home_src,
    homes,
    out,
    inbox,
    ans_out,
    ans_in,
    base,
    limits,
    mixed,
    local_sem,
    w_sem,
    home_send,
    home_recv,
    row_send,
    row_recv,
    ans_send,
    ans_recv,
):
    me = lax.axis_index("replica")
    heads = features // HEAD
    parts = 16 // MOST
    cols = width // parts
    per_row = steps * heads
    half = peers // 2
    w_parts = w_sem.shape[0]
    w_rows = width // w_parts

    def offset(i):
        return lax.rem(peers // 2 + (1 - 2 * lax.rem(i, 2)) * ((i + 1) // 2) + peers, peers)

    def target(i):
        return lax.rem(me + offset(i), peers)

    def source(i):
        return lax.rem(me - offset(i) + peers, peers)

    def w_copy(c):
        piece = pl.ds(c * w_rows, w_rows)
        return pltpu.make_async_copy(w_hbm.at[piece], w.at[piece], w_sem.at[c])

    x_copy = pltpu.make_async_copy(x_hbm, x, local_sem.at[0])
    shrink_copy = pltpu.make_async_copy(shrink_hbm, shrink, local_sem.at[1])
    k_copy = pltpu.make_async_copy(k_hbm, k, local_sem.at[2])
    v_copy = pltpu.make_async_copy(v_hbm, v, local_sem.at[3])

    home_local = pltpu.make_async_copy(home_hbm, home_ref, local_sem.at[4])
    ids_copy = pltpu.make_async_copy(ids_hbm, ids_ref, local_sem.at[5])
    len_copy = pltpu.make_async_copy(len_hbm, len_ref, local_sem.at[6])
    expand_copy = pltpu.make_async_copy(expand_hbm, expand_ref, local_sem.at[7])

    barrier = pltpu.get_barrier_semaphore()

    @pl.loop(0, peers - 1)
    def _(i):
        pl.semaphore_signal(barrier, inc=1, device_id={"replica": target(i)}, device_id_type=MESH)

    home_local.start()
    ids_copy.start()
    x_copy.start()

    home_local.wait()
    home_src[...] = jnp.full(home_src.shape, home_ref[0], jnp.int32)
    homes[me] = home_src[...]

    def home_copy(i, slot):
        return pltpu.make_async_remote_copy(
            src_ref=home_src,
            dst_ref=homes.at[slot],
            send_sem=home_send.at[i],
            recv_sem=home_recv.at[slot],
            device_id={"replica": target(i)},
            device_id_type=MESH,
        )

    pl.semaphore_wait(barrier, peers - 1)

    @pl.loop(0, peers - 1)
    def _(i):
        home_copy(i, me).start()

    for c in range(w_parts):
        w_copy(c).start()
    shrink_copy.start()
    k_copy.start()
    v_copy.start()
    len_copy.start()
    expand_copy.start()

    total = steps * rows
    ids_copy.wait()
    same = iota((rows, rows), 0) == iota((rows, rows), 1)
    ids_col = jnp.concatenate(
        [
            jnp.sum(jnp.where(same, ids_ref[s].astype(F32), 0.0), axis=1, keepdims=True)
            for s in range(steps)
        ],
        axis=0,
    )

    def along(col, index):
        return jnp.sum(jnp.where(iota((total, index.shape[1]), 0) == index, col, 0.0), axis=0, keepdims=True)

    ids_row = along(ids_col, iota((1, total), 1))
    before = (iota((total, total), 1) < iota((total, total), 0)) & (
        iota((total, total), 1) // rows == iota((total, total), 0) // rows
    )
    place_col = jnp.sum(jnp.where(before & (ids_row == ids_col), 1.0, 0.0), axis=1, keepdims=True)
    lanes = iota((1, parts * rows), 1)
    pack_ids = [along(ids_col, lanes % rows + s * rows) for s in range(steps)]
    pack_place = [along(place_col, lanes % rows + s * rows) for s in range(steps)]
    block = iota((peers * 16, 1), 0)
    pack_target = target(block // 16)
    fits = [
        (block % parts == lanes // rows) & ((block // parts) % MOST == pack_place[s].astype(jnp.int32))
        for s in range(steps)
    ]
    x_copy.wait()

    @pl.loop(0, peers - 1)
    def _(i):
        home_copy(i, source(i)).wait_recv()

    home_col = jnp.max(homes[...], axis=1)[:, 0:1].astype(F32)

    def owner_of(ids):
        named = iota((peers, ids.shape[1]), 0) == ids.astype(jnp.int32)
        return jnp.sum(jnp.where(named, home_col, 0.0), axis=0, keepdims=True).astype(jnp.int32)

    def row_copy(s, i):
        place = pl.ds(s * 16, 16)
        return pltpu.make_async_remote_copy(
            src_ref=out.at[i, place],
            dst_ref=inbox.at[i, place],
            send_sem=row_send.at[s, i],
            recv_sem=row_recv.at[s, i],
            device_id={"replica": target(i)},
            device_id_type=MESH,
        )

    for s in range(steps):
        routing = jnp.where(fits[s] & (pack_target == owner_of(pack_ids[s])), 1.0, 0.0).astype(BF16)
        tall = jnp.concatenate([x[s, :, c * cols : (c + 1) * cols] for c in range(parts)], axis=0)
        for g in range(2):
            packed = jnp.dot(
                routing[g * half * 16 : (g + 1) * half * 16], tall, preferred_element_type=F32
            ).astype(BF16)
            packed = packed.reshape(half, 16, cols)
            out[g * half : (g + 1) * half, s * 16 : (s + 1) * 16, :] = packed
            if g == 1:
                inbox[peers - 1, s * 16 : (s + 1) * 16, :] = packed[half - 1]

            @pl.loop(g * half, min((g + 1) * half, peers - 1))
            def _(i):
                row_copy(s, i).start()

    q_lanes = iota((1, rows * per_row), 1)
    q_rows = q_lanes // per_row + ((q_lanes // heads) % steps) * rows
    q_owner = owner_of(along(ids_col, q_rows))
    q_place = along(place_col, q_rows).astype(jnp.int32)
    a_rows = iota((peers * steps * MOST * heads, 1), 0)
    per_peer = steps * MOST * heads
    back = (
        (target(a_rows // per_peer) == q_owner)
        & ((a_rows // (MOST * heads)) % steps == (q_lanes // heads) % steps)
        & ((a_rows // heads) % MOST == q_place)
        & (a_rows % heads == q_lanes % heads)
    )
    back = jnp.transpose(jnp.where(back, 1.0, 0.0)).astype(BF16)

    flat = jnp.zeros((total, features), F32)
    for c in range(w_parts):
        w_copy(c).wait()
        piece = x[:, :, c * w_rows : (c + 1) * w_rows].reshape(total, w_rows)
        flat = flat + jnp.dot(piece, w[c * w_rows : (c + 1) * w_rows], preferred_element_type=F32)
    for s in range(steps):
        for h in range(heads):
            base[pl.ds(s * heads + h, rows, stride=per_row), :] = flat[
                s * rows : (s + 1) * rows, h * HEAD : (h + 1) * HEAD
            ]
    step_of = iota((per_row, ctx), 0) // heads
    len_copy.wait()
    for t in range(rows):
        limits[t] = step_of + len_ref[t]
    shrink_copy.wait()
    for c in range(parts):
        wide[c * rank : (c + 1) * rank] = shrink[0, :, c * cols : (c + 1) * cols]
    expand_copy.wait()
    expand = expand_ref[0]
    expand_tall = jnp.concatenate([expand[:, h * HEAD : (h + 1) * HEAD] for h in range(heads)], axis=0)
    k_copy.wait()
    v_copy.wait()

    g_rows = half * 16
    own_part = iota((g_rows, parts * rank), 0) % parts == iota((g_rows, parts * rank), 1) // rank

    def low_rank(s, g):
        block = inbox[g * half : (g + 1) * half, s * 16 : (s + 1) * 16, :].reshape(g_rows, cols)
        full = lax.dot_general(block, wide[...], (((1,), (1,)), ((), ())), preferred_element_type=F32)
        full = jnp.where(own_part, full, 0.0).reshape(g_rows // parts, parts, parts * rank)
        full = jnp.sum(full, axis=1)
        while full.shape[1] > 2 * rank:
            full = full[:, : full.shape[1] // 2] + full[:, full.shape[1] // 2 :]
        return (full + pltpu.roll(full, rank, 1)).astype(BF16)

    def wait_rows(s, g):
        @pl.loop(g * half, min((g + 1) * half, peers - 1))
        def _(i):
            row_copy(s, i).wait_recv()

    def answer_copy(i, to):
        return pltpu.make_async_remote_copy(
            src_ref=ans_out.at[i],
            dst_ref=ans_in.at[i],
            send_sem=ans_send.at[i],
            recv_sem=ans_recv.at[i],
            device_id={"replica": to},
            device_id_type=MESH,
        )

    lows = {}
    r_rows = half * per_peer
    r_from = iota((r_rows, steps * half * MOST), 1)
    r_to = iota((r_rows, steps * half * MOST), 0)
    spread = (
        ((r_to // (MOST * heads)) % steps == r_from // (half * MOST))
        & (r_to // per_peer == (r_from // MOST) % half)
        & ((r_to // heads) % MOST == r_from % MOST)
    )
    spread = jnp.where(spread, 1.0, 0.0).astype(BF16)
    own_head = iota((r_rows, heads * rank), 0) % heads == iota((r_rows, heads * rank), 1) // rank
    for s in range(steps):
        for g in (0, 1):
            wait_rows(s, g)
            lows[s, g] = low_rank(s, g)
            if s < steps - 1:
                continue
            low = jnp.concatenate([lows[q, g] for q in range(steps)], axis=0)
            low = jnp.concatenate([low] * (heads // 2), axis=1)
            low = jnp.dot(spread, low, preferred_element_type=F32)
            low = jnp.where(own_head, low, 0.0).astype(BF16)
            answer = jnp.dot(low, expand_tall, preferred_element_type=F32).astype(BF16)
            answer = answer.reshape(half, per_peer, HEAD)
            ans_out[g * half : (g + 1) * half] = answer
            if g == 1:
                ans_in[peers - 1] = answer[half - 1]

            @pl.loop(g * half, min((g + 1) * half, peers - 1))
            def _(i):
                answer_copy(i, source(i)).start()

    @pl.loop(0, peers - 1)
    def _(i):
        home_copy(i, me).wait_send()
        for s in range(steps):
            row_copy(s, i).wait_send()
        answer_copy(i, source(i)).wait_send()

    @pl.loop(0, peers - 1)
    def _(i):
        answer_copy(i, source(i)).wait_recv()

    delta = jnp.dot(back, ans_in[...].reshape(peers * per_peer, HEAD), preferred_element_type=F32)
    query = (base[...] + delta).astype(BF16).reshape(rows, per_row, HEAD)
    scores = lax.dot_general(query, k[...], (((2,), (2,)), ((0,), (0,))), preferred_element_type=F32)
    scores = scores * HEAD ** (-0.5)
    scores = jnp.where(iota((rows, per_row, ctx), 2) < limits[...], scores, -1e30)
    weights = jnp.exp(scores - jnp.max(scores, axis=-1, keepdims=True))
    weights = (weights / jnp.sum(weights, axis=-1, keepdims=True)).astype(BF16)
    result = lax.dot_general(weights, v[...], (((2,), (1,)), ((0,), (0,))), preferred_element_type=F32)
    mixed[...] = result.reshape(rows * per_row, HEAD)
    for s in range(steps):
        for h in range(heads):
            o_ref[s, :, h * HEAD : (h + 1) * HEAD] = mixed[
                pl.ds(s * heads + h, rows, stride=per_row), :
            ].astype(BF16)


def body(inputs, query_weight, key_cache, value_cache, cache_len, ids, home, shrink_pool, expand_pool):
    peers = lax.axis_size("replica")
    steps, rows, width = inputs.shape
    features = query_weight.shape[1]
    rank = shrink_pool.shape[2]
    ctx = key_cache.shape[1]
    heads = features // HEAD
    cols = width * MOST // 16
    per_row = steps * heads
    vmem = pl.BlockSpec(memory_space=pltpu.VMEM)
    hbm = pl.BlockSpec(memory_space=pltpu.HBM)
    dma = pltpu.SemaphoreType.DMA
    return pl.pallas_call(
        functools.partial(kernel, peers, steps, rows, width, rank, features, ctx),
        out_shape=jax.ShapeDtypeStruct((steps, rows, features), BF16),
        in_specs=[hbm] * 9,
        out_specs=vmem,
        scratch_shapes=[
            pltpu.VMEM(inputs.shape, BF16),
            pltpu.VMEM(query_weight.shape, BF16),
            pltpu.VMEM(key_cache.shape, BF16),
            pltpu.VMEM(value_cache.shape, BF16),
            pltpu.SMEM(cache_len.shape, jnp.int32),
            pltpu.VMEM((steps, 1, rows), jnp.int32),
            pltpu.SMEM(home.shape, jnp.int32),
            pltpu.VMEM((1, rank, width), BF16),
            pltpu.VMEM(expand_pool.shape, BF16),
            pltpu.VMEM((rank * 16 // MOST, cols), BF16),
            pltpu.VMEM((1, 128), jnp.int32),
            pltpu.VMEM((peers, 1, 128), jnp.int32),
            pltpu.VMEM((peers, steps * 16, cols), BF16),
            pltpu.VMEM((peers, steps * 16, cols), BF16),
            pltpu.VMEM((peers, steps * MOST * heads, HEAD), BF16),
            pltpu.VMEM((peers, steps * MOST * heads, HEAD), BF16),
            pltpu.VMEM((rows * per_row, HEAD), F32),
            pltpu.VMEM((rows, per_row, ctx), jnp.int32),
            pltpu.VMEM((rows * per_row, HEAD), F32),
            dma((8,)),
            dma((8,)),
            dma((peers,)),
            dma((peers,)),
            dma((steps, peers)),
            dma((steps, peers)),
            dma((peers,)),
            dma((peers,)),
        ],
        compiler_params=pltpu.CompilerParams(
            collective_id=0, has_side_effects=True, vmem_limit_bytes=60 * 2**20
        ),
    )(
        inputs,
        query_weight,
        key_cache,
        value_cache,
        cache_len,
        jnp.swapaxes(ids, 1, 2),
        home,
        jnp.swapaxes(shrink_pool, 1, 2),
        expand_pool,
    )


def solution(mesh):
    return jax.shard_map(
        body,
        mesh=mesh,
        in_specs=(
            P(None, ("groups", "replica"), None),
            P(),
            P(("groups", "replica"), None, None),
            P(("groups", "replica"), None, None),
            P(("groups", "replica")),
            P(None, ("groups", "replica"), None),
            P("replica"),
            P("replica", None, None),
            P("replica", None, None),
        ),
        out_specs=P(None, ("groups", "replica"), None),
        check_vma=False,
    )
```

```python
import functools

import jax
import jax.numpy as jnp
from jax import lax
from jax.experimental import pallas as pl
from jax.experimental.pallas import tpu as pltpu
from jax.sharding import PartitionSpec as P

HEAD = 128
MOST = 2
MESH = pl.DeviceIdType.MESH
F32 = jnp.float32
BF16 = jnp.bfloat16


def iota(shape, axis):
    return lax.broadcasted_iota(jnp.int32, shape, axis)


def kernel(
    peers,
    steps,
    rows,
    width,
    rank,
    features,
    ctx,
    x_hbm,
    w_hbm,
    k_hbm,
    v_hbm,
    len_hbm,
    ids_hbm,
    home_hbm,
    shrink_hbm,
    expand_hbm,
    o_ref,
    x,
    w,
    k,
    v,
    len_ref,
    ids_ref,
    home_ref,
    shrink,
    expand_ref,
    wide,
    home_src,
    homes,
    out,
    inbox,
    ans_out,
    ans_in,
    base,
    limits,
    mixed,
    local_sem,
    w_sem,
    home_send,
    home_recv,
    row_send,
    row_recv,
    ans_send,
    ans_recv,
):
    me = lax.axis_index("replica")
    heads = features // HEAD
    parts = 16 // MOST
    cols = width // parts
    per_row = steps * heads
    share = peers
    w_parts = w_sem.shape[0]
    w_rows = width // w_parts

    def offset(i):
        return lax.rem(peers // 2 + (1 - 2 * lax.rem(i, 2)) * ((i + 1) // 2) + peers, peers)

    def target(i):
        return lax.rem(me + offset(i), peers)

    def source(i):
        return lax.rem(me - offset(i) + peers, peers)

    def w_copy(c):
        piece = pl.ds(c * w_rows, w_rows)
        return pltpu.make_async_copy(w_hbm.at[piece], w.at[piece], w_sem.at[c])

    x_copy = pltpu.make_async_copy(x_hbm, x, local_sem.at[0])
    shrink_copy = pltpu.make_async_copy(shrink_hbm, shrink, local_sem.at[1])
    k_copy = pltpu.make_async_copy(k_hbm, k, local_sem.at[2])
    v_copy = pltpu.make_async_copy(v_hbm, v, local_sem.at[3])

    home_local = pltpu.make_async_copy(home_hbm, home_ref, local_sem.at[4])
    ids_copy = pltpu.make_async_copy(ids_hbm, ids_ref, local_sem.at[5])
    len_copy = pltpu.make_async_copy(len_hbm, len_ref, local_sem.at[6])
    expand_copy = pltpu.make_async_copy(expand_hbm, expand_ref, local_sem.at[7])

    barrier = pltpu.get_barrier_semaphore()

    @pl.loop(0, peers - 1)
    def _(i):
        pl.semaphore_signal(barrier, inc=1, device_id={"replica": target(i)}, device_id_type=MESH)

    home_local.start()
    ids_copy.start()
    x_copy.start()

    home_local.wait()
    home_src[...] = jnp.full(home_src.shape, home_ref[0], jnp.int32)
    homes[me] = home_src[...]

    def home_copy(i, slot):
        return pltpu.make_async_remote_copy(
            src_ref=home_src,
            dst_ref=homes.at[slot],
            send_sem=home_send.at[i],
            recv_sem=home_recv.at[slot],
            device_id={"replica": target(i)},
            device_id_type=MESH,
        )

    pl.semaphore_wait(barrier, peers - 1)

    @pl.loop(0, peers - 1)
    def _(i):
        home_copy(i, me).start()

    for c in range(w_parts):
        w_copy(c).start()
    shrink_copy.start()
    k_copy.start()
    v_copy.start()
    len_copy.start()
    expand_copy.start()

    total = steps * rows
    ids_copy.wait()
    same = iota((rows, rows), 0) == iota((rows, rows), 1)
    ids_col = jnp.concatenate(
        [
            jnp.sum(jnp.where(same, ids_ref[s].astype(F32), 0.0), axis=1, keepdims=True)
            for s in range(steps)
        ],
        axis=0,
    )

    def along(col, index):
        return jnp.sum(jnp.where(iota((total, index.shape[1]), 0) == index, col, 0.0), axis=0, keepdims=True)

    ids_row = along(ids_col, iota((1, total), 1))
    before = (iota((total, total), 1) < iota((total, total), 0)) & (
        iota((total, total), 1) // rows == iota((total, total), 0) // rows
    )
    place_col = jnp.sum(jnp.where(before & (ids_row == ids_col), 1.0, 0.0), axis=1, keepdims=True)
    lanes = iota((1, parts * rows), 1)
    pack_ids = [along(ids_col, lanes % rows + s * rows) for s in range(steps)]
    pack_place = [along(place_col, lanes % rows + s * rows) for s in range(steps)]
    block = iota((peers * 16, 1), 0)
    pack_target = target(block // 16)
    fits = [
        (block % parts == lanes // rows) & ((block // parts) % MOST == pack_place[s].astype(jnp.int32))
        for s in range(steps)
    ]
    x_copy.wait()

    @pl.loop(0, peers - 1)
    def _(i):
        home_copy(i, source(i)).wait_recv()

    home_col = jnp.max(homes[...], axis=1)[:, 0:1].astype(F32)

    def owner_of(ids):
        named = iota((peers, ids.shape[1]), 0) == ids.astype(jnp.int32)
        return jnp.sum(jnp.where(named, home_col, 0.0), axis=0, keepdims=True).astype(jnp.int32)

    def row_copy(s, i):
        place = pl.ds(s * 16, 16)
        return pltpu.make_async_remote_copy(
            src_ref=out.at[i, place],
            dst_ref=inbox.at[i, place],
            send_sem=row_send.at[s, i],
            recv_sem=row_recv.at[s, i],
            device_id={"replica": target(i)},
            device_id_type=MESH,
        )

    for s in range(steps):
        routing = jnp.where(fits[s] & (pack_target == owner_of(pack_ids[s])), 1.0, 0.0).astype(BF16)
        tall = jnp.concatenate([x[s, :, c * cols : (c + 1) * cols] for c in range(parts)], axis=0)
        for g in range(1):
            packed = jnp.dot(
                routing[g * share * 16 : (g + 1) * share * 16], tall, preferred_element_type=F32
            ).astype(BF16)
            packed = packed.reshape(share, 16, cols)
            out[g * share : (g + 1) * share, s * 16 : (s + 1) * 16, :] = packed
            if g == 0:
                inbox[peers - 1, s * 16 : (s + 1) * 16, :] = packed[share - 1]

            @pl.loop(g * share, min((g + 1) * share, peers - 1))
            def _(i):
                row_copy(s, i).start()

    q_lanes = iota((1, rows * per_row), 1)
    q_rows = q_lanes // per_row + ((q_lanes // heads) % steps) * rows
    q_owner = owner_of(along(ids_col, q_rows))
    q_place = along(place_col, q_rows).astype(jnp.int32)
    a_rows = iota((peers * steps * MOST * heads, 1), 0)
    per_peer = steps * MOST * heads
    back = (
        (target(a_rows // per_peer) == q_owner)
        & ((a_rows // (MOST * heads)) % steps == (q_lanes // heads) % steps)
        & ((a_rows // heads) % MOST == q_place)
        & (a_rows % heads == q_lanes % heads)
    )
    back = jnp.transpose(jnp.where(back, 1.0, 0.0)).astype(BF16)

    flat = jnp.zeros((total, features), F32)
    for c in range(w_parts):
        w_copy(c).wait()
        piece = x[:, :, c * w_rows : (c + 1) * w_rows].reshape(total, w_rows)
        flat = flat + jnp.dot(piece, w[c * w_rows : (c + 1) * w_rows], preferred_element_type=F32)
    for s in range(steps):
        for h in range(heads):
            base[pl.ds(s * heads + h, rows, stride=per_row), :] = flat[
                s * rows : (s + 1) * rows, h * HEAD : (h + 1) * HEAD
            ]
    step_of = iota((per_row, ctx), 0) // heads
    len_copy.wait()
    for t in range(rows):
        limits[t] = step_of + len_ref[t]
    shrink_copy.wait()
    for c in range(parts):
        wide[c * rank : (c + 1) * rank] = shrink[0, :, c * cols : (c + 1) * cols]
    expand_copy.wait()
    expand = expand_ref[0]
    expand_tall = jnp.concatenate([expand[:, h * HEAD : (h + 1) * HEAD] for h in range(heads)], axis=0)
    k_copy.wait()
    v_copy.wait()

    g_rows = share * 16
    own_part = iota((g_rows, parts * rank), 0) % parts == iota((g_rows, parts * rank), 1) // rank

    def low_rank(s, g):
        block = inbox[g * share : (g + 1) * share, s * 16 : (s + 1) * 16, :].reshape(g_rows, cols)
        full = lax.dot_general(block, wide[...], (((1,), (1,)), ((), ())), preferred_element_type=F32)
        full = jnp.where(own_part, full, 0.0).reshape(g_rows // parts, parts, parts * rank)
        full = jnp.sum(full, axis=1)
        while full.shape[1] > 2 * rank:
            full = full[:, : full.shape[1] // 2] + full[:, full.shape[1] // 2 :]
        return (full + pltpu.roll(full, rank, 1)).astype(BF16)

    def wait_rows(s, g):
        @pl.loop(g * share, min((g + 1) * share, peers - 1))
        def _(i):
            row_copy(s, i).wait_recv()

    def answer_copy(i, to):
        return pltpu.make_async_remote_copy(
            src_ref=ans_out.at[i],
            dst_ref=ans_in.at[i],
            send_sem=ans_send.at[i],
            recv_sem=ans_recv.at[i],
            device_id={"replica": to},
            device_id_type=MESH,
        )

    lows = {}
    r_rows = share * per_peer
    r_from = iota((r_rows, steps * share * MOST), 1)
    r_to = iota((r_rows, steps * share * MOST), 0)
    spread = (
        ((r_to // (MOST * heads)) % steps == r_from // (share * MOST))
        & (r_to // per_peer == (r_from // MOST) % share)
        & ((r_to // heads) % MOST == r_from % MOST)
    )
    spread = jnp.where(spread, 1.0, 0.0).astype(BF16)
    own_head = iota((r_rows, heads * rank), 0) % heads == iota((r_rows, heads * rank), 1) // rank
    for s in range(steps):
        for g in range(1):
            wait_rows(s, g)
            lows[s, g] = low_rank(s, g)
            if s < steps - 1:
                continue
            low = jnp.concatenate([lows[q, g] for q in range(steps)], axis=0)
            low = jnp.concatenate([low] * (heads // 2), axis=1)
            low = jnp.dot(spread, low, preferred_element_type=F32)
            low = jnp.where(own_head, low, 0.0).astype(BF16)
            answer = jnp.dot(low, expand_tall, preferred_element_type=F32).astype(BF16)
            answer = answer.reshape(share, per_peer, HEAD)
            ans_out[g * share : (g + 1) * share] = answer
            if g == 0:
                ans_in[peers - 1] = answer[share - 1]

            @pl.loop(g * share, min((g + 1) * share, peers - 1))
            def _(i):
                answer_copy(i, source(i)).start()

    @pl.loop(0, peers - 1)
    def _(i):
        home_copy(i, me).wait_send()
        for s in range(steps):
            row_copy(s, i).wait_send()
        answer_copy(i, source(i)).wait_send()

    @pl.loop(0, peers - 1)
    def _(i):
        answer_copy(i, source(i)).wait_recv()

    delta = jnp.dot(back, ans_in[...].reshape(peers * per_peer, HEAD), preferred_element_type=F32)
    query = (base[...] + delta).astype(BF16).reshape(rows, per_row, HEAD)
    scores = lax.dot_general(query, k[...], (((2,), (2,)), ((0,), (0,))), preferred_element_type=F32)
    scores = scores * HEAD ** (-0.5)
    scores = jnp.where(iota((rows, per_row, ctx), 2) < limits[...], scores, -1e30)
    weights = jnp.exp(scores - jnp.max(scores, axis=-1, keepdims=True))
    weights = (weights / jnp.sum(weights, axis=-1, keepdims=True)).astype(BF16)
    result = lax.dot_general(weights, v[...], (((2,), (1,)), ((0,), (0,))), preferred_element_type=F32)
    mixed[...] = result.reshape(rows * per_row, HEAD)
    for s in range(steps):
        for h in range(heads):
            o_ref[s, :, h * HEAD : (h + 1) * HEAD] = mixed[
                pl.ds(s * heads + h, rows, stride=per_row), :
            ].astype(BF16)


def body(inputs, query_weight, key_cache, value_cache, cache_len, ids, home, shrink_pool, expand_pool):
    peers = lax.axis_size("replica")
    steps, rows, width = inputs.shape
    features = query_weight.shape[1]
    rank = shrink_pool.shape[2]
    ctx = key_cache.shape[1]
    heads = features // HEAD
    cols = width * MOST // 16
    per_row = steps * heads
    vmem = pl.BlockSpec(memory_space=pltpu.VMEM)
    hbm = pl.BlockSpec(memory_space=pltpu.HBM)
    dma = pltpu.SemaphoreType.DMA
    return pl.pallas_call(
        functools.partial(kernel, peers, steps, rows, width, rank, features, ctx),
        out_shape=jax.ShapeDtypeStruct((steps, rows, features), BF16),
        in_specs=[hbm] * 9,
        out_specs=vmem,
        scratch_shapes=[
            pltpu.VMEM(inputs.shape, BF16),
            pltpu.VMEM(query_weight.shape, BF16),
            pltpu.VMEM(key_cache.shape, BF16),
            pltpu.VMEM(value_cache.shape, BF16),
            pltpu.SMEM(cache_len.shape, jnp.int32),
            pltpu.VMEM((steps, 1, rows), jnp.int32),
            pltpu.SMEM(home.shape, jnp.int32),
            pltpu.VMEM((1, rank, width), BF16),
            pltpu.VMEM(expand_pool.shape, BF16),
            pltpu.VMEM((rank * 16 // MOST, cols), BF16),
            pltpu.VMEM((1, 128), jnp.int32),
            pltpu.VMEM((peers, 1, 128), jnp.int32),
            pltpu.VMEM((peers, steps * 16, cols), BF16),
            pltpu.VMEM((peers, steps * 16, cols), BF16),
            pltpu.VMEM((peers, steps * MOST * heads, HEAD), BF16),
            pltpu.VMEM((peers, steps * MOST * heads, HEAD), BF16),
            pltpu.VMEM((rows * per_row, HEAD), F32),
            pltpu.VMEM((rows, per_row, ctx), jnp.int32),
            pltpu.VMEM((rows * per_row, HEAD), F32),
            dma((8,)),
            dma((8,)),
            dma((peers,)),
            dma((peers,)),
            dma((steps, peers)),
            dma((steps, peers)),
            dma((peers,)),
            dma((peers,)),
        ],
        compiler_params=pltpu.CompilerParams(
            collective_id=0, has_side_effects=True, vmem_limit_bytes=60 * 2**20
        ),
    )(
        inputs,
        query_weight,
        key_cache,
        value_cache,
        cache_len,
        jnp.swapaxes(ids, 1, 2),
        home,
        jnp.swapaxes(shrink_pool, 1, 2),
        expand_pool,
    )


def solution(mesh):
    return jax.shard_map(
        body,
        mesh=mesh,
        in_specs=(
            P(None, ("groups", "replica"), None),
            P(),
            P(("groups", "replica"), None, None),
            P(("groups", "replica"), None, None),
            P(("groups", "replica")),
            P(None, ("groups", "replica"), None),
            P("replica"),
            P("replica", None, None),
            P("replica", None, None),
        ),
        out_specs=P(None, ("groups", "replica"), None),
        check_vma=False,
    )
```
